128 devices in a mesh: layer: 4 (over z_lo, core), latent: 32 (over x, z_hi, y).
Axes of the slice: x: 4, y: 4, z: 4 (z_hi: 2, z_lo: 2; z = z_hi * 2 + z_lo), core: 2. Of those that a mesh axis runs over, the one named last changes fastest.
Arguments:
- residuals: bfloat16 [4, 512, 3584], P('layer', 'latent'), may hold values from -6 to 6
- enc_weight: bfloat16 [4, 3584, 24576], P('layer', None, 'latent'), may hold values from -0.046875 to 0.046875
- dec_weight: bfloat16 [4, 24576, 3584], P('layer', 'latent'), may hold values from -0.0390625 to 0.0390625
- enc_bias: float32 [24576], P('latent'), may hold values from -1 to 0.5
- dec_bias: float32 [4, 3584], P('layer'), may hold values from -3 to 3
Outputs:
- enc_grad: bfloat16 [4, 3584, 24576], P('layer', None, 'latent')
- dec_grad: bfloat16 [4, 24576, 3584], P('layer', 'latent')
- enc_bias_grad: float32 [24576], P('latent')
The draws below stay inside these ranges and needn't reach their ends.
All inputs are finite; a program needn't handle non-finite values.
Results may differ from the reference program's by a relative error of at most 0.02.
Values may be sent and summed in bfloat16 or wider, within the bound.
No kernel may reach another device: no remote copies, remote signals or barrier semaphores. Data moves between devices by JAX's collectives and lax.ppermute only.
A program may use at most 128 MiB of HBM per device.

```python
import jax
import jax.numpy as jnp
from jax import lax

D = 3584
LAYERS = 4
LATENTS = 24576
TOKENS = 512


def levels(rng, extent, cuts, low, top_value):
    gain = 1.0
    for dim, shards_of in cuts:
        steps = jax.random.uniform(jax.random.fold_in(jax.random.fold_in(rng, 6), dim), (shards_of,), jnp.float32, low / len(cuts), top_value / len(cuts))
        gain = gain * jnp.repeat(jnp.exp(steps), extent[dim] // shards_of).reshape((-1,) + (1,) * (len(extent) - 1 - dim))
    return gain


def centred(key, extent, scale, bound, pieces=(), dtype=jnp.bfloat16):
    result = jax.random.normal(key, extent, jnp.float32) * scale
    if len(pieces) > 0:
        result = levels(key, extent, pieces, -0.22, 0.18) * result
    return jnp.clip(result, min=-bound, max=bound).astype(dtype)


def setup_inputs(seed: int = 0) -> dict:
    keys = jax.random.split(jax.random.key(seed), 6)
    residuals = centred(keys[0], (LAYERS, TOKENS, D), 1.0, 6.0, ((0, 4), (1, 32)))
    enc_weight = centred(keys[1], (LAYERS, D, LATENTS), (LAYERS * D) ** -0.5, 0.046875, ((0, 4), (2, 32)))
    dec_weight = centred(keys[2], (LAYERS, LATENTS, D), LATENTS ** -0.5, 0.0390625, ((0, 4), (1, 32)))
    enc_bias = jnp.clip(-1.0 + 1.5 * jax.random.uniform(keys[3], (LATENTS,), jnp.float32) ** levels(keys[3], (LATENTS,), ((0, 32),), -0.2, 0.2), -1.0, 0.5)
    dec_bias = centred(keys[4], (LAYERS, D), 0.5, 3.0, ((0, 4),), jnp.float32)
    return {"residuals": residuals, "enc_weight": enc_weight, "dec_weight": dec_weight, "enc_bias": enc_bias, "dec_bias": dec_bias}


sparsity_weight = 0.5
sharpness = 4.0

def reference(residuals, enc_weight, dec_weight, enc_bias, dec_bias):
    pre = enc_bias[None, :].astype(jnp.float32)
    for level in range(LAYERS):
        pre = pre + jnp.dot(residuals[level], enc_weight[level], preferred_element_type=jnp.float32)
    latents = (jax.nn.softplus(sharpness * pre) / sharpness).astype(jnp.bfloat16)
    gate_all = jax.nn.sigmoid(sharpness * pre)
    norm_list = []
    for level in range(LAYERS):
        squares = lax.optimization_barrier(jnp.sum(jnp.square(dec_weight[level].astype(jnp.float32)), axis=1))
        norm_list.append(jnp.sqrt(squares + 1e-06))
    weight_sum = norm_list[0]
    for level in range(1, LAYERS):
        weight_sum = weight_sum + norm_list[level]
    act_sum = lax.optimization_barrier(jnp.sum(latents.astype(jnp.float32), axis=0))
    lat_part = jnp.zeros((TOKENS, LATENTS), jnp.float32)
    dec_list = []
    for level in range(LAYERS):
        rebuilt = jnp.dot(latents, dec_weight[level], preferred_element_type=jnp.float32)
        misfit = rebuilt + dec_bias[level][None, :] - residuals[level].astype(jnp.float32)
        err_grad = (2.0 * misfit).astype(jnp.bfloat16)
        lat_part = lat_part + lax.dot_general(err_grad, dec_weight[level], (((1,), (1,)), ((), ())), preferred_element_type=jnp.float32)
        main_term = lax.dot_general(latents, err_grad, (((0,), (0,)), ((), ())), preferred_element_type=jnp.float32)
        penalty_term = sparsity_weight * act_sum[:, None] * dec_weight[level].astype(jnp.float32) / norm_list[level][:, None]
        dec_list.append((main_term + penalty_term).astype(jnp.bfloat16))
    lat_grad = lat_part + sparsity_weight * weight_sum[None, :]
    pre_grad = (lat_grad * gate_all).astype(jnp.bfloat16)
    enc_list = []
    for level in range(LAYERS):
        enc_list.append(lax.dot_general(residuals[level], pre_grad, (((0,), (0,)), ((), ())), preferred_element_type=jnp.float32).astype(jnp.bfloat16))
    enc_bias_grad = lax.optimization_barrier(jnp.sum(pre_grad.astype(jnp.float32), axis=0))
    return (jnp.stack(enc_list), jnp.stack(dec_list), enc_bias_grad)
```

```python
import jax
import jax.numpy as jnp
from jax import lax
from jax.sharding import PartitionSpec as P

sparsity_weight = 0.5
sharpness = 4.0

SIZES = {"x": 4, "zh": 2, "y": 4}
STRIDES = {"x": 8, "zh": 4, "y": 1}


def latent_shift(value, axis, by):
    size, stride = SIZES[axis], STRIDES[axis]
    pairs = []
    for i in range(32):
        at = i // stride % size
        pairs.append((i, i + ((at + by) % size - at) * stride))
    return lax.ppermute(value, "latent", pairs)


def layer_swap(value, bit):
    return lax.ppermute(value, "layer", [(i, i ^ bit) for i in range(4)])


def gather_rows(rows, first, second):
    rows = jnp.concatenate([rows, latent_shift(rows, "zh", 1)], axis=0)
    for axis in (first, second):
        rows = jnp.concatenate([rows] + [latent_shift(rows, axis, -k) for k in (1, 2, 3)], axis=0)
    return rows


def scatter_sum(rows, first, second):
    for axis, size in ((second, 4), (first, 4), ("zh", 2)):
        step = rows.shape[0] // size
        total = rows[:step].astype(jnp.float32)
        for k in range(1, size):
            got = latent_shift(rows[k * step : (k + 1) * step], axis, k)
            total = total + got.astype(jnp.float32)
        rows = total if axis == "zh" else total.astype(jnp.bfloat16)
    return rows


def layer_scatter(part, upper_core, upper_z):
    half = part.shape[0] // 2
    low, high = part[:half], part[half:]
    keep, send = jnp.where(upper_core, high, low), jnp.where(upper_core, low, high)
    part = keep + layer_swap(send, 1)
    half //= 2
    low, high = part[:half], part[half:]
    keep, send = jnp.where(upper_z, high, low), jnp.where(upper_z, low, high)
    return keep + layer_swap(send.astype(jnp.bfloat16), 2).astype(jnp.float32)


def layer_gather(rows, upper_core, upper_z):
    for upper, bit in ((upper_z, 2), (upper_core, 1)):
        other = layer_swap(rows, bit)
        rows = jnp.concatenate(
            [jnp.where(upper, other, rows), jnp.where(upper, rows, other)], axis=0
        )
    return rows


def per_device(residuals, enc_weight, dec_weight, enc_bias, dec_bias):
    own_rows = residuals[0]
    enc_local = enc_weight[0]
    dec_local = dec_weight[0]
    layer = lax.axis_index("layer")
    upper_core, upper_z = layer % 2 == 1, layer >= 2

    row_norms = jnp.sqrt(jnp.sum(jnp.square(dec_local.astype(jnp.float32)), axis=1) + 1e-06)
    weight_sum = row_norms + layer_swap(row_norms, 1)
    weight_sum = weight_sum + layer_swap(weight_sum, 2)
    penalty = sparsity_weight * weight_sum[None, :]

    ways = (("y", "x"), ("x", "y"))
    halves = [own_rows[:8], own_rows[8:]]
    gathered = [gather_rows(h, *w) for h, w in zip(halves, ways)]
    latents, gates, errors, pre_grads = [], [], [], []
    for part in range(2):
        pre = jnp.dot(gathered[part], enc_local, preferred_element_type=jnp.float32)
        pre = layer_scatter(pre, upper_core, upper_z) + enc_bias[None, :]
        lat = (jax.nn.softplus(sharpness * pre) / sharpness).astype(jnp.bfloat16)
        gates.append(jax.nn.sigmoid(sharpness * pre))
        latents.append(layer_gather(lat, upper_core, upper_z))
    for part in range(2):
        rebuilt = jnp.dot(latents[part], dec_local, preferred_element_type=jnp.float32)
        rebuilt = scatter_sum(rebuilt.astype(jnp.bfloat16), *ways[part])
        misfit = rebuilt + dec_bias[0][None, :] - halves[part].astype(jnp.float32)
        error = (2.0 * misfit).astype(jnp.bfloat16)
        errors.append(gather_rows(error, *ways[part]))
    for part in range(2):
        back = lax.dot_general(
            errors[part], dec_local, (((1,), (1,)), ((), ())), preferred_element_type=jnp.float32
        )
        lat_grad = layer_scatter(back, upper_core, upper_z) + penalty
        pre_grads.append(
            layer_gather((lat_grad * gates[part]).astype(jnp.bfloat16), upper_core, upper_z)
        )
    all_latents = jnp.concatenate(latents, axis=0)
    act_sum = jnp.sum(all_latents.astype(jnp.float32), axis=0)
    dec_acc = lax.dot_general(
        all_latents,
        jnp.concatenate(errors, axis=0),
        (((0,), (0,)), ((), ())),
        preferred_element_type=jnp.float32,
    )
    penalty_term = (
        sparsity_weight * act_sum[:, None] * dec_local.astype(jnp.float32) / row_norms[:, None]
    )
    dec_grad = (dec_acc + penalty_term).astype(jnp.bfloat16)
    pre_grad = jnp.concatenate(pre_grads, axis=0)
    enc_grad = lax.dot_general(
        jnp.concatenate(gathered, axis=0),
        pre_grad,
        (((0,), (0,)), ((), ())),
        preferred_element_type=jnp.float32,
    ).astype(jnp.bfloat16)
    enc_bias_grad = jnp.sum(pre_grad.astype(jnp.float32), axis=0)
    return (enc_grad[None], dec_grad[None], enc_bias_grad)


def solution(mesh):
    in_specs = (
        P("layer", "latent", None),
        P("layer", None, "latent"),
        P("layer", "latent", None),
        P("latent"),
        P("layer", None),
    )
    out_specs = (P("layer", None, "latent"), P("layer", "latent", None), P("latent"))
    return jax.shard_map(
        per_device, mesh=mesh, in_specs=in_specs, out_specs=out_specs, check_vma=False
    )
```

```python
import jax
import jax.numpy as jnp
from jax import lax
from jax.sharding import PartitionSpec as P

sparsity_weight = 0.5
sharpness = 4.0

SIZES = {"x": 4, "zh": 2, "y": 4}
STRIDES = {"x": 8, "zh": 4, "y": 1}
ORDER = (("y", "x"), ("x", "y"))


def shift(value, slot, stage, by):
    pairs = []
    for layer in range(4):
        axis = "zh" if stage == "zh" else ORDER[(layer + slot) % 2][stage]
        size, stride = SIZES[axis], STRIDES[axis]
        for i in range(32):
            at = i // stride % size
            pairs.append((layer * 32 + i, layer * 32 + i + ((at + by) % size - at) * stride))
    return lax.ppermute(value, ("layer", "latent"), pairs)


def layer_swap(value, bit):
    return lax.ppermute(value, "layer", [(i, i ^ bit) for i in range(4)])


def join(*rows):
    return jnp.concatenate(rows, axis=0)


def rounded(value):
    return lax.reduce_precision(value, 8, 7)


def wide(value):
    return value.astype(jnp.float32)


def narrow(value):
    return value.astype(jnp.bfloat16)


def ring_gather(rows, slot, stage):
    half = rows.shape[0] // 2
    after, before = shift(rows, slot, stage, -1), shift(rows, slot, stage, 1)
    far = shift(after[:half], slot, stage, -1), shift(before[half:], slot, stage, 1)
    return join(rows, after, *far, before)


def near_gather(rows, slot, stage):
    far, after, before = (shift(rows, slot, stage, by) for by in (2, -1, 1))
    return join(rows, after, far, before)


def ring_scatter(rows, slot, stage):
    n = rows.shape[0] // 4
    half = n // 2
    up = shift(rows[n + half : 2 * n + half], slot, stage, 1)
    down = shift(rows[2 * n + half : 3 * n + half], slot, stage, -1)
    up_far = narrow(wide(rows[n : n + half]) + wide(up[half:]))
    down_far = narrow(wide(rows[3 * n + half :]) + wide(down[:half]))
    up_far, down_far = shift(up_far, slot, stage, 1), shift(down_far, slot, stage, -1)
    return (
        wide(rows[:n])
        + join(wide(up_far), wide(up[:half]))
        + join(wide(down[half:]), wide(down_far))
    )


def near_scatter(rows, slot, stage):
    n = rows.shape[0] // 4
    total = wide(rows[:n])
    for k in (2, 1, 3):
        total = total + wide(shift(rows[k * n : (k + 1) * n], slot, stage, k))
    return total


def gather_rows(pair, slot):
    return ring_gather(near_gather(pair, slot, 0), slot, 1)


def scatter_sum(rows, slot):
    pair = rounded(near_scatter(narrow(ring_scatter(rows, slot, 1)), slot, 0))
    other = wide(shift(narrow(pair), slot, "zh", 1))
    half = pair.shape[0] // 2
    return pair + join(other[half:], other[:half])


def layer_sum(keep, send):
    part = rounded(keep + layer_swap(send, 1))
    return part + wide(layer_swap(narrow(part), 2))


def per_device(residuals, enc_weight, dec_weight, enc_bias, dec_bias):
    own_rows = residuals[0]
    enc_local = enc_weight[0]
    dec_local = dec_weight[0]
    upper = lax.axis_index("layer") % 2 == 1

    row_norms = jnp.sqrt(jnp.sum(jnp.square(wide(dec_local)), axis=1) + 1e-06)
    weight_sum = row_norms + layer_swap(row_norms, 1)
    weight_sum = weight_sum + layer_swap(weight_sum, 2)
    penalty = sparsity_weight * weight_sum[None, :]

    other_rows = shift(own_rows, 0, "zh", 1)
    low, high = join(own_rows[:8], other_rows[:8]), join(own_rows[8:], other_rows[8:])
    pairs = [jnp.where(upper, high, low), jnp.where(upper, low, high)]
    gathered = [gather_rows(pairs[slot], slot) for slot in (0, 1)]
    gathered = list(lax.optimization_barrier(tuple(gathered)))
    pre = [jnp.dot(rows, enc_local, preferred_element_type=jnp.float32) for rows in gathered]
    pre = layer_sum(*pre) + enc_bias[None, :]
    kept = narrow(jax.nn.softplus(sharpness * pre) / sharpness)
    gate = jax.nn.sigmoid(sharpness * pre)
    latents = [kept, layer_swap(kept, 1)]
    latents = list(lax.optimization_barrier(tuple(latents)))
    errors = []
    for slot in (0, 1):
        rebuilt = jnp.dot(latents[slot], dec_local, preferred_element_type=jnp.float32)
        rebuilt = scatter_sum(narrow(rebuilt), slot)
        misfit = rebuilt + dec_bias[0][None, :] - wide(pairs[slot])
        errors.append(narrow(2.0 * misfit))
    errors = list(lax.optimization_barrier(tuple(errors)))
    errors = [gather_rows(errors[slot], slot) for slot in (0, 1)]
    errors = list(lax.optimization_barrier(tuple(errors)))
    back = [
        lax.dot_general(
            rows, dec_local, (((1,), (1,)), ((), ())), preferred_element_type=jnp.float32
        )
        for rows in errors
    ]
    lat_grad = layer_sum(*back) + penalty
    kept = narrow(lat_grad * gate)
    pre_grads = [kept, layer_swap(kept, 1)]
    act_sum = jnp.sum(wide(join(*latents)), axis=0)
    dec_acc = lax.dot_general(
        join(*latents),
        join(*errors),
        (((0,), (0,)), ((), ())),
        preferred_element_type=jnp.float32,
    )
    penalty_term = sparsity_weight * act_sum[:, None] * wide(dec_local) / row_norms[:, None]
    dec_grad = narrow(dec_acc + penalty_term)
    enc_grad = narrow(
        lax.dot_general(
            join(*gathered),
            join(*pre_grads),
            (((0,), (0,)), ((), ())),
            preferred_element_type=jnp.float32,
        )
    )
    enc_bias_grad = jnp.sum(wide(pre_grads[0]), axis=0) + jnp.sum(wide(pre_grads[1]), axis=0)
    return (enc_grad[None], dec_grad[None], enc_bias_grad)


def solution(mesh):
    in_specs = (
        P("layer", "latent", None),
        P("layer", None, "latent"),
        P("layer", "latent", None),
        P("latent"),
        P("layer", None),
    )
    out_specs = (P("layer", None, "latent"), P("layer", "latent", None), P("latent"))
    return jax.shard_map(
        per_device, mesh=mesh, in_specs=in_specs, out_specs=out_specs, check_vma=False
    )
```

```python
import jax
import jax.numpy as jnp
from jax import lax
from jax.sharding import PartitionSpec as P

sparsity_weight = 0.5
sharpness = 4.0

SIZES = {"x": 4, "zh": 2, "y": 4}
STRIDES = {"x": 8, "zh": 4, "y": 1}
ORDER = (("y", "x"), ("x", "y"))


def shift(value, slot, stage, by):
    pairs = []
    for layer in range(4):
        axis = "zh" if stage == "zh" else ORDER[(layer + slot) % 2][stage]
        size, stride = SIZES[axis], STRIDES[axis]
        for i in range(32):
            at = i // stride % size
            pairs.append((layer * 32 + i, layer * 32 + i + ((at + by) % size - at) * stride))
    return lax.ppermute(value, ("layer", "latent"), pairs)


def layer_swap(value, bit):
    return lax.ppermute(value, "layer", [(i, i ^ bit) for i in range(4)])


def join(*rows):
    return jnp.concatenate(rows, axis=0)


def rounded(value):
    return lax.reduce_precision(value, 8, 7)


def wide(value):
    return value.astype(jnp.float32)


def narrow(value):
    return value.astype(jnp.bfloat16)


def ring_gather(rows, slot, stage):
    half = rows.shape[0] // 2
    after, before = shift(rows, slot, stage, -1), shift(rows, slot, stage, 1)
    far = shift(after[:half], slot, stage, -1), shift(before[half:], slot, stage, 1)
    return join(rows, after, *far, before)


def near_gather(rows, slot, stage):
    far, after, before = (shift(rows, slot, stage, by) for by in (2, -1, 1))
    return join(rows, after, far, before)


def ring_scatter(rows, slot, stage):
    n = rows.shape[0] // 4
    half = n // 2
    up = shift(rows[n + half : 2 * n + half], slot, stage, 1)
    down = shift(rows[2 * n + half : 3 * n + half], slot, stage, -1)
    up_far = narrow(wide(rows[n : n + half]) + wide(up[half:]))
    down_far = narrow(wide(rows[3 * n + half :]) + wide(down[:half]))
    up_far, down_far = shift(up_far, slot, stage, 1), shift(down_far, slot, stage, -1)
    return (
        wide(rows[:n])
        + join(wide(up_far), wide(up[:half]))
        + join(wide(down[half:]), wide(down_far))
    )


def near_scatter(rows, slot, stage):
    n = rows.shape[0] // 4
    total = wide(rows[:n])
    for k in (2, 1, 3):
        total = total + wide(shift(rows[k * n : (k + 1) * n], slot, stage, k))
    return total


def gather_rows(pair, slot):
    return ring_gather(near_gather(pair, slot, 0), slot, 1)


def scatter_sum(rows, slot):
    pair = rounded(near_scatter(narrow(ring_scatter(rows, slot, 1)), slot, 0))
    other = wide(shift(narrow(pair), slot, "zh", 1))
    half = pair.shape[0] // 2
    return pair + join(other[half:], other[:half])


def core_sum(keep, send):
    return rounded(lax.optimization_barrier(keep) + layer_swap(send, 1))


def per_device(residuals, enc_weight, dec_weight, enc_bias, dec_bias):
    own_rows = residuals[0]
    enc_local = enc_weight[0]
    dec_local = dec_weight[0]
    upper = lax.axis_index("layer") % 2 == 1

    other_rows = shift(own_rows, 0, "zh", 1)
    low, high = join(own_rows[:8], other_rows[:8]), join(own_rows[8:], other_rows[8:])
    pairs = [jnp.where(upper, high, low), jnp.where(upper, low, high)]
    gathered = [gather_rows(pairs[slot], slot) for slot in (0, 1)]
    gathered = list(lax.optimization_barrier(tuple(gathered)))
    pre = [jnp.dot(rows, enc_local, preferred_element_type=jnp.float32) for rows in gathered]
    part = core_sum(*pre)
    other = layer_swap(narrow(part), 2)
    part, dec_local = lax.optimization_barrier((part, dec_local))
    row_norms = jnp.sqrt(jnp.sum(jnp.square(wide(dec_local)), axis=1) + 1e-06)
    other, row_norms = lax.optimization_barrier((other, row_norms))
    pre = part + wide(other) + enc_bias[None, :]
    kept = narrow(jax.nn.softplus(sharpness * pre) / sharpness)
    gate = jax.nn.sigmoid(sharpness * pre)
    latents = [kept, layer_swap(kept, 1)]
    latents = list(lax.optimization_barrier(tuple(latents)))
    errors = []
    for slot in (0, 1):
        rebuilt = jnp.dot(latents[slot], dec_local, preferred_element_type=jnp.float32)
        rebuilt = scatter_sum(narrow(rebuilt), slot)
        misfit = rebuilt + dec_bias[0][None, :] - wide(pairs[slot])
        errors.append(narrow(2.0 * misfit))
    errors = [gather_rows(errors[slot], slot) for slot in (0, 1)]
    errors = list(lax.optimization_barrier(tuple(errors)))
    back = [
        lax.dot_general(
            rows, dec_local, (((1,), (1,)), ((), ())), preferred_element_type=jnp.float32
        )
        for rows in errors
    ]
    norm_rows = jnp.broadcast_to(row_norms[None, :], (8, row_norms.shape[0]))
    got = layer_swap(join(back[1], norm_rows), 1)
    part = rounded(lax.optimization_barrier(back[0]) + got[:256])
    chip_norms = row_norms + got[256]
    head = rounded(chip_norms)
    tail = rounded(chip_norms - head)
    norm_rows = jnp.where(jnp.arange(8)[:, None] < 4, head[None, :], tail[None, :])
    other = layer_swap(narrow(join(part, norm_rows)), 2)
    act_sum = jnp.sum(wide(join(*latents)), axis=0)
    dec_acc = lax.dot_general(
        join(*latents),
        join(*errors),
        (((0,), (0,)), ((), ())),
        preferred_element_type=jnp.float32,
    )
    penalty_term = sparsity_weight * act_sum[:, None] * wide(dec_local) / row_norms[:, None]
    dec_grad = narrow(dec_acc + penalty_term)
    other, dec_grad = lax.optimization_barrier((other, dec_grad))
    weight_sum = (head + tail) + (wide(other[256]) + wide(other[260]))
    lat_grad = part + wide(other[:256]) + sparsity_weight * weight_sum[None, :]
    kept = narrow(lat_grad * gate)
    pre_grads = [kept, layer_swap(kept, 1)]
    enc_grad = narrow(
        lax.dot_general(
            join(*gathered),
            join(*pre_grads),
            (((0,), (0,)), ((), ())),
            preferred_element_type=jnp.float32,
        )
    )
    enc_bias_grad = jnp.sum(wide(pre_grads[0]), axis=0) + jnp.sum(wide(pre_grads[1]), axis=0)
    return (enc_grad[None], dec_grad[None], enc_bias_grad)


def solution(mesh):
    in_specs = (
        P("layer", "latent", None),
        P("layer", None, "latent"),
        P("layer", "latent", None),
        P("latent"),
        P("layer", None),
    )
    out_specs = (P("layer", None, "latent"), P("layer", "latent", None), P("latent"))
    return jax.shard_map(
        per_device, mesh=mesh, in_specs=in_specs, out_specs=out_specs, check_vma=False
    )
```

```python
import jax
import jax.numpy as jnp
from jax import lax
from jax.sharding import PartitionSpec as P

sparsity_weight = 0.5
sharpness = 4.0

SIZES = {"x": 4, "zh": 2, "y": 4}
STRIDES = {"x": 8, "zh": 4, "y": 1}
ORDER = (("y", "x"), ("x", "y"))


def shift(value, slot, stage, by):
    pairs = []
    for layer in range(4):
        axis = "zh" if stage == "zh" else ORDER[(layer + slot) % 2][stage]
        size, stride = SIZES[axis], STRIDES[axis]
        for i in range(32):
            at = i // stride % size
            pairs.append((layer * 32 + i, layer * 32 + i + ((at + by) % size - at) * stride))
    return lax.ppermute(value, ("layer", "latent"), pairs)


def layer_swap(value, bit):
    return lax.ppermute(value, "layer", [(i, i ^ bit) for i in range(4)])


def join(*rows):
    return jnp.concatenate(rows, axis=0)


def rounded(value):
    return lax.reduce_precision(value, 8, 7)


def wide(value):
    return value.astype(jnp.float32)


def narrow(value):
    return value.astype(jnp.bfloat16)


def ring_gather(rows, slot, stage):
    half = rows.shape[0] // 2
    after, before = shift(rows, slot, stage, -1), shift(rows, slot, stage, 1)
    far = shift(after[:half], slot, stage, -1), shift(before[half:], slot, stage, 1)
    return join(rows, after, *far, before)


def near_gather(rows, slot, stage):
    far, after, before = (shift(rows, slot, stage, by) for by in (2, -1, 1))
    return join(rows, after, far, before)


def ring_scatter(rows, slot, stage):
    n = rows.shape[0] // 4
    half = n // 2
    up = shift(rows[n + half : 2 * n + half], slot, stage, 1)
    down = shift(rows[2 * n + half : 3 * n + half], slot, stage, -1)
    up_far = narrow(wide(rows[n : n + half]) + wide(up[half:]))
    down_far = narrow(wide(rows[3 * n + half :]) + wide(down[:half]))
    up_far, down_far = shift(up_far, slot, stage, 1), shift(down_far, slot, stage, -1)
    return (
        wide(rows[:n])
        + join(wide(up_far), wide(up[:half]))
        + join(wide(down[half:]), wide(down_far))
    )


def near_scatter(rows, slot, stage):
    n = rows.shape[0] // 4
    total = wide(rows[:n])
    for k in (2, 1, 3):
        total = total + wide(shift(rows[k * n : (k + 1) * n], slot, stage, k))
    return total


def gather_rows(pair, slot):
    return ring_gather(near_gather(pair, slot, 0), slot, 1)


def scatter_sum(rows, slot):
    pair = rounded(near_scatter(narrow(ring_scatter(rows, slot, 1)), slot, 0))
    other = wide(shift(narrow(pair), slot, "zh", 1))
    half = pair.shape[0] // 2
    return pair + join(other[half:], other[:half])


def core_sum(keep, send):
    return rounded(lax.optimization_barrier(keep) + wide(layer_swap(narrow(send), 1)))


def per_device(residuals, enc_weight, dec_weight, enc_bias, dec_bias):
    own_rows = residuals[0]
    enc_local = enc_weight[0]
    dec_local = dec_weight[0]
    upper = lax.axis_index("layer") % 2 == 1

    other_rows = shift(own_rows, 0, "zh", 1)
    low, high = join(own_rows[:8], other_rows[:8]), join(own_rows[8:], other_rows[8:])
    pairs = [jnp.where(upper, high, low), jnp.where(upper, low, high)]
    gathered = [gather_rows(pairs[slot], slot) for slot in (0, 1)]
    gathered = list(lax.optimization_barrier(tuple(gathered)))
    pre = [jnp.dot(rows, enc_local, preferred_element_type=jnp.float32) for rows in gathered]
    part = core_sum(*pre)
    other = layer_swap(narrow(part), 2)
    part, dec_local = lax.optimization_barrier((part, dec_local))
    row_norms = jnp.sqrt(jnp.sum(jnp.square(wide(dec_local)), axis=1) + 1e-06)
    other, row_norms = lax.optimization_barrier((other, row_norms))
    pre = part + wide(other) + enc_bias[None, :]
    kept = narrow(jax.nn.softplus(sharpness * pre) / sharpness)
    gate = jax.nn.sigmoid(sharpness * pre)
    latents = [kept, layer_swap(kept, 1)]
    latents = list(lax.optimization_barrier(tuple(latents)))
    errors = []
    for slot in (0, 1):
        rebuilt = jnp.dot(latents[slot], dec_local, preferred_element_type=jnp.float32)
        rebuilt = scatter_sum(narrow(rebuilt), slot)
        misfit = rebuilt + dec_bias[0][None, :] - wide(pairs[slot])
        errors.append(narrow(2.0 * misfit))
    errors = [gather_rows(errors[slot], slot) for slot in (0, 1)]
    errors = list(lax.optimization_barrier(tuple(errors)))
    back = [
        lax.dot_general(
            rows, dec_local, (((1,), (1,)), ((), ())), preferred_element_type=jnp.float32
        )
        for rows in errors
    ]
    def norm_rows(norms):
        head = rounded(norms)
        tail = rounded(norms - head)
        return jnp.where(jnp.arange(8)[:, None] < 4, head[None, :], tail[None, :]), head + tail

    extra, norms = norm_rows(row_norms)
    got = layer_swap(narrow(join(back[1], extra)), 1)
    part = rounded(lax.optimization_barrier(back[0]) + wide(got[:256]))
    extra, norms = norm_rows(norms + (wide(got[256]) + wide(got[260])))
    other = layer_swap(narrow(join(part, extra)), 2)
    act_sum = jnp.sum(wide(join(*latents)), axis=0)
    dec_acc = lax.dot_general(
        join(*latents),
        join(*errors),
        (((0,), (0,)), ((), ())),
        preferred_element_type=jnp.float32,
    )
    penalty_term = sparsity_weight * act_sum[:, None] * wide(dec_local) / row_norms[:, None]
    dec_grad = narrow(dec_acc + penalty_term)
    other, dec_grad = lax.optimization_barrier((other, dec_grad))
    weight_sum = norms + (wide(other[256]) + wide(other[260]))
    lat_grad = part + wide(other[:256]) + sparsity_weight * weight_sum[None, :]
    kept = narrow(lat_grad * gate)
    pre_grads = [kept, layer_swap(kept, 1)]
    enc_grad = narrow(
        lax.dot_general(
            join(*gathered),
            join(*pre_grads),
            (((0,), (0,)), ((), ())),
            preferred_element_type=jnp.float32,
        )
    )
    enc_bias_grad = jnp.sum(wide(pre_grads[0]), axis=0) + jnp.sum(wide(pre_grads[1]), axis=0)
    return (enc_grad[None], dec_grad[None], enc_bias_grad)


def solution(mesh):
    in_specs = (
        P("layer", "latent", None),
        P("layer", None, "latent"),
        P("layer", "latent", None),
        P("latent"),
        P("layer", None),
    )
    out_specs = (P("layer", None, "latent"), P("layer", "latent", None), P("latent"))
    return jax.shard_map(
        per_device, mesh=mesh, in_specs=in_specs, out_specs=out_specs, check_vma=False
    )
```

```python
import jax
import jax.numpy as jnp
from jax import lax
from jax.sharding import PartitionSpec as P

sparsity_weight = 0.5
sharpness = 4.0

SIZES = {"x": 4, "zh": 2, "y": 4}
STRIDES = {"x": 8, "zh": 4, "y": 1}
ORDER = (("y", "x"), ("x", "y"))


def shift(value, slot, stage, by):
    pairs = []
    for layer in range(4):
        axis = "zh" if stage == "zh" else ORDER[(layer + slot) % 2][stage]
        size, stride = SIZES[axis], STRIDES[axis]
        for i in range(32):
            at = i // stride % size
            pairs.append((layer * 32 + i, layer * 32 + i + ((at + by) % size - at) * stride))
    return lax.ppermute(value, ("layer", "latent"), pairs)


def layer_swap(value, bit):
    return lax.ppermute(value, "layer", [(i, i ^ bit) for i in range(4)])


def join(*rows):
    return jnp.concatenate(rows, axis=0)


def rounded(value):
    return lax.reduce_precision(value, 8, 7)


def wide(value):
    return value.astype(jnp.float32)


def narrow(value):
    return value.astype(jnp.bfloat16)


def ring_gather(rows, slot, stage):
    half = rows.shape[0] // 2
    after, before = shift(rows, slot, stage, -1), shift(rows, slot, stage, 1)
    far = shift(after[:half], slot, stage, -1), shift(before[half:], slot, stage, 1)
    return join(rows, after, *far, before)


def near_gather(rows, slot, stage):
    far, after, before = (shift(rows, slot, stage, by) for by in (2, -1, 1))
    return join(rows, after, far, before)


def ring_scatter(first, second, slot, stage):
    n = first.shape[0] // 2
    half = n // 2
    up = shift(first[:n], slot, stage, 1)
    down = shift(first[n:], slot, stage, -1)
    up_far = narrow(wide(second[n : n + half]) + wide(up[half:]))
    down_far = narrow(wide(second[n + half :]) + wide(down[:half]))
    up_far, down_far = shift(up_far, slot, stage, 1), shift(down_far, slot, stage, -1)
    return (
        wide(second[:n])
        + join(wide(up_far), wide(up[:half]))
        + join(wide(down[half:]), wide(down_far))
    )


def near_scatter(rows, slot, stage):
    n = rows.shape[0] // 4
    total = wide(rows[:n])
    for k in (2, 1, 3):
        total = total + wide(shift(rows[k * n : (k + 1) * n], slot, stage, k))
    return total


def gather_rows(pair, slot):
    return ring_gather(near_gather(pair, slot, 0), slot, 1)


def scatter_sum(first, second, slot):
    pair = rounded(near_scatter(narrow(ring_scatter(first, second, slot, 1)), slot, 0))
    other = wide(shift(narrow(pair), slot, "zh", 1))
    half = pair.shape[0] // 2
    return pair + join(other[half:], other[:half])


def core_sum(keep, send):
    return rounded(lax.optimization_barrier(keep) + wide(layer_swap(narrow(send), 1)))


def per_device(residuals, enc_weight, dec_weight, enc_bias, dec_bias):
    own_rows = residuals[0]
    enc_local = enc_weight[0]
    dec_local = dec_weight[0]
    upper = lax.axis_index("layer") % 2 == 1

    other_rows = shift(own_rows, 0, "zh", 1)
    low, high = join(own_rows[:8], other_rows[:8]), join(own_rows[8:], other_rows[8:])
    pairs = [jnp.where(upper, high, low), jnp.where(upper, low, high)]
    gathered = [gather_rows(pairs[slot], slot) for slot in (0, 1)]
    pre = [jnp.dot(rows, enc_local, preferred_element_type=jnp.float32) for rows in gathered]
    part = core_sum(*pre)
    first, second = part[96:224], join(part[:96], part[224:])
    other = [layer_swap(narrow(rows), 2) for rows in (first, second)]
    part, dec_local = lax.optimization_barrier((part, dec_local))
    row_norms = jnp.sqrt(jnp.sum(jnp.square(wide(dec_local)), axis=1) + 1e-06)
    other[0], row_norms = lax.optimization_barrier((other[0], row_norms))
    dec_copy = dec_local
    gates, latents, products = [], [], []
    for rows in (first, second):
        got = other[len(gates)]
        pre = rows + wide(got) + enc_bias[None, :]
        gates.append(jax.nn.sigmoid(sharpness * pre))
        kept = narrow(jax.nn.softplus(sharpness * pre) / sharpness)
        latents.append((kept, layer_swap(kept, 1)))
        products.append(
            [
                narrow(jnp.dot(rows, dec_copy, preferred_element_type=jnp.float32))
                for rows in latents[-1]
            ]
        )
        if len(gates) == 1:
            other[1], products[0] = lax.optimization_barrier((other[1], products[0]))
    gate = join(gates[1][:96], gates[0], gates[1][96:])
    latents = [join(b[:96], a, b[96:]) for a, b in zip(*latents)]
    errors = []
    for slot in (0, 1):
        rebuilt = scatter_sum(products[0][slot], products[1][slot], slot)
        misfit = rebuilt + dec_bias[0][None, :] - wide(pairs[slot])
        errors.append(narrow(2.0 * misfit))
    errors = [gather_rows(errors[slot], slot) for slot in (0, 1)]
    errors = list(lax.optimization_barrier(tuple(errors)))
    back = [
        lax.dot_general(
            rows, dec_local, (((1,), (1,)), ((), ())), preferred_element_type=jnp.float32
        )
        for rows in errors
    ]
    def norm_rows(norms):
        head = rounded(norms)
        tail = rounded(norms - head)
        return jnp.where(jnp.arange(8)[:, None] < 4, head[None, :], tail[None, :]), head + tail

    extra, norms = norm_rows(row_norms)
    got = layer_swap(narrow(join(back[1], extra)), 1)
    part = rounded(lax.optimization_barrier(back[0]) + wide(got[:256]))
    extra, norms = norm_rows(norms + (wide(got[256]) + wide(got[260])))
    other = layer_swap(narrow(join(part, extra)), 2)
    act_sum = jnp.sum(wide(join(*latents)), axis=0)
    dec_acc = lax.dot_general(
        join(*latents),
        join(*errors),
        (((0,), (0,)), ((), ())),
        preferred_element_type=jnp.float32,
    )
    penalty_term = sparsity_weight * act_sum[:, None] * wide(dec_local) / row_norms[:, None]
    dec_grad = narrow(dec_acc + penalty_term)
    other, dec_grad = lax.optimization_barrier((other, dec_grad))
    weight_sum = norms + (wide(other[256]) + wide(other[260]))
    lat_grad = part + wide(other[:256]) + sparsity_weight * weight_sum[None, :]
    kept = narrow(lat_grad * gate)
    pre_grads = [kept, layer_swap(kept, 1)]
    enc_grad = narrow(
        lax.dot_general(
            join(*gathered),
            join(*pre_grads),
            (((0,), (0,)), ((), ())),
            preferred_element_type=jnp.float32,
        )
    )
    enc_bias_grad = jnp.sum(wide(pre_grads[0]), axis=0) + jnp.sum(wide(pre_grads[1]), axis=0)
    return (enc_grad[None], dec_grad[None], enc_bias_grad)


def solution(mesh):
    in_specs = (
        P("layer", "latent", None),
        P("layer", None, "latent"),
        P("layer", "latent", None),
        P("latent"),
        P("layer", None),
    )
    out_specs = (P("layer", None, "latent"), P("layer", "latent", None), P("latent"))
    return jax.shard_map(
        per_device, mesh=mesh, in_specs=in_specs, out_specs=out_specs, check_vma=False
    )
```

```python
import jax
import jax.numpy as jnp
from jax import lax
from jax.sharding import PartitionSpec as P

sparsity_weight = 0.5
sharpness = 4.0

SIZES = {"x": 4, "zh": 2, "y": 4}
STRIDES = {"x": 8, "zh": 4, "y": 1}
ORDER = (("y", "x"), ("x", "y"))


def shift(value, slot, stage, by):
    pairs = []
    for layer in range(4):
        axis = "zh" if stage == "zh" else ORDER[(layer + slot) % 2][stage]
        size, stride = SIZES[axis], STRIDES[axis]
        for i in range(32):
            at = i // stride % size
            pairs.append((layer * 32 + i, layer * 32 + i + ((at + by) % size - at) * stride))
    return lax.ppermute(value, ("layer", "latent"), pairs)


def layer_swap(value, bit):
    return lax.ppermute(value, "layer", [(i, i ^ bit) for i in range(4)])


def join(*rows):
    return jnp.concatenate(rows, axis=0)


def rounded(value):
    return lax.reduce_precision(value, 8, 7)


def wide(value):
    return value.astype(jnp.float32)


def narrow(value):
    return value.astype(jnp.bfloat16)


def ring_gather(rows, slot, stage):
    half = rows.shape[0] // 2
    after, before = shift(rows, slot, stage, -1), shift(rows, slot, stage, 1)
    far = shift(after[:half], slot, stage, -1), shift(before[half:], slot, stage, 1)
    return join(rows, after, *far, before)


def near_gather(rows, slot, stage):
    far, after, before = (shift(rows, slot, stage, by) for by in (2, -1, 1))
    return join(rows, after, far, before)


def ring_scatter(first, second, slot, stage):
    n = first.shape[0] // 2
    half = n // 2
    up = shift(first[:n], slot, stage, 1)
    down = shift(first[n:], slot, stage, -1)
    up_far = narrow(wide(second[n : n + half]) + wide(up[half:]))
    down_far = narrow(wide(second[n + half :]) + wide(down[:half]))
    up_far, down_far = shift(up_far, slot, stage, 1), shift(down_far, slot, stage, -1)
    return (
        wide(second[:n])
        + join(wide(up_far), wide(up[:half]))
        + join(wide(down[half:]), wide(down_far))
    )


def near_scatter(rows, slot, stage):
    n = rows.shape[0] // 4
    total = wide(rows[:n])
    for k in (2, 1, 3):
        total = total + wide(shift(rows[k * n : (k + 1) * n], slot, stage, k))
    return total


def gather_rows(pair, slot):
    return ring_gather(near_gather(pair, slot, 0), slot, 1)


def scatter_sum(first, second, slot):
    pair = rounded(near_scatter(narrow(ring_scatter(first, second, slot, 1)), slot, 0))
    other = wide(shift(narrow(pair), slot, "zh", 1))
    half = pair.shape[0] // 2
    return pair + join(other[half:], other[:half])


def core_sum(keep, send):
    return rounded(lax.optimization_barrier(keep) + wide(layer_swap(narrow(send), 1)))


def per_device(residuals, enc_weight, dec_weight, enc_bias, dec_bias):
    own_rows = residuals[0]
    enc_local = enc_weight[0]
    dec_local = dec_weight[0]
    upper = lax.axis_index("layer") % 2 == 1

    other_rows = shift(own_rows, 0, "zh", 1)
    low, high = join(own_rows[:8], other_rows[:8]), join(own_rows[8:], other_rows[8:])
    pairs = [jnp.where(upper, high, low), jnp.where(upper, low, high)]
    gathered = [gather_rows(pairs[slot], slot) for slot in (0, 1)]
    pre = [jnp.dot(rows, enc_local, preferred_element_type=jnp.float32) for rows in gathered]
    part = core_sum(*pre)
    first, second = part[96:224], join(part[:96], part[224:])
    other = [layer_swap(narrow(rows), 2) for rows in (first, second)]
    part, dec_local = lax.optimization_barrier((part, dec_local))
    row_norms = jnp.sqrt(jnp.sum(jnp.square(wide(dec_local)), axis=1) + 1e-06)
    other[0], row_norms = lax.optimization_barrier((other[0], row_norms))
    dec_copy = dec_local
    gates, latents, products = [], [], []
    for rows in (first, second):
        got = other[len(gates)]
        pre = rows + wide(got) + enc_bias[None, :]
        gates.append(jax.nn.sigmoid(sharpness * pre))
        kept = narrow(jax.nn.softplus(sharpness * pre) / sharpness)
        latents.append((kept, layer_swap(kept, 1)))
        products.append(
            [
                narrow(jnp.dot(rows, dec_copy, preferred_element_type=jnp.float32))
                for rows in latents[-1]
            ]
        )
        if len(gates) == 1:
            other[1], products[0] = lax.optimization_barrier((other[1], products[0]))
    gate = join(gates[1][:96], gates[0], gates[1][96:])
    latents = [join(b[:96], a, b[96:]) for a, b in zip(*latents)]
    errors = []
    for slot in (0, 1):
        rebuilt = scatter_sum(products[0][slot], products[1][slot], slot)
        misfit = rebuilt + dec_bias[0][None, :] - wide(pairs[slot])
        errors.append(narrow(2.0 * misfit))
    errors = [gather_rows(errors[slot], slot) for slot in (0, 1)]
    back = [None, None]
    for slot in (1, 0):
        back[slot] = lax.dot_general(
            errors[slot], dec_local, (((1,), (1,)), ((), ())), preferred_element_type=jnp.float32
        )
        if slot == 1:
            errors[0], back[1] = lax.optimization_barrier((errors[0], back[1]))
    def norm_rows(norms):
        head = rounded(norms)
        tail = rounded(norms - head)
        return jnp.where(jnp.arange(8)[:, None] < 4, head[None, :], tail[None, :]), head + tail

    extra, norms = norm_rows(row_norms)
    got = layer_swap(narrow(join(back[1], extra)), 1)
    part = rounded(lax.optimization_barrier(back[0]) + wide(got[:256]))
    extra, norms = norm_rows(norms + (wide(got[256]) + wide(got[260])))
    other = layer_swap(narrow(join(part, extra)), 2)
    act_sum = jnp.sum(wide(join(*latents)), axis=0)
    dec_acc = lax.dot_general(
        join(*latents),
        join(*errors),
        (((0,), (0,)), ((), ())),
        preferred_element_type=jnp.float32,
    )
    penalty_term = sparsity_weight * act_sum[:, None] * wide(dec_local) / row_norms[:, None]
    dec_grad = narrow(dec_acc + penalty_term)
    other, dec_grad = lax.optimization_barrier((other, dec_grad))
    weight_sum = norms + (wide(other[256]) + wide(other[260]))
    lat_grad = part + wide(other[:256]) + sparsity_weight * weight_sum[None, :]
    kept = narrow(lat_grad * gate)
    pre_grads = [kept, layer_swap(kept, 1)]
    enc_grad = narrow(
        lax.dot_general(
            join(*gathered),
            join(*pre_grads),
            (((0,), (0,)), ((), ())),
            preferred_element_type=jnp.float32,
        )
    )
    enc_bias_grad = jnp.sum(wide(pre_grads[0]), axis=0) + jnp.sum(wide(pre_grads[1]), axis=0)
    return (enc_grad[None], dec_grad[None], enc_bias_grad)


def solution(mesh):
    in_specs = (
        P("layer", "latent", None),
        P("layer", None, "latent"),
        P("layer", "latent", None),
        P("latent"),
        P("layer", None),
    )
    out_specs = (P("layer", None, "latent"), P("layer", "latent", None), P("latent"))
    return jax.shard_map(
        per_device, mesh=mesh, in_specs=in_specs, out_specs=out_specs, check_vma=False
    )
```
